512 devices in a mesh: dp: 32 (over z, core), tensor: 16 (over x, y).
Axes of the slice: x: 4, y: 4, z: 16, core: 2. Of those that a mesh axis runs over, the one named last changes fastest.
Arguments:
- hidden_acts: bfloat16 [12288, 28672], P('dp', 'tensor'), may hold values from -6 to 6
- out_grads: bfloat16 [12288, 8192], P('dp', 'tensor'), may hold values from -6 to 6
- query_left: bfloat16 [1024, 28672], P('dp', 'tensor'), may hold values from -10 to 10, as said below
- query_right: bfloat16 [1024, 8192], P('dp', 'tensor'), may hold values from -10 to 10, as said below
Outputs:
- influence: float32 [32, 12288], P(None, 'dp')
The draws below stay inside these ranges and needn't reach their ends.
Inputs may be any that keep to these rules, and one draw needn't show every extreme that they name: `query_left`: rows q * 32 to q * 32 + 31 are the hidden-unit factors of query q. `query_right`: rows q * 32 to q * 32 + 31 are the model-width factors of query q.
All inputs are finite; a program needn't handle non-finite values.
Results may differ from the reference program's by a relative error of at most 0.0003.
Values may be sent and summed in bfloat16 or wider, within the bound.
No kernel may reach another device: no remote copies, remote signals or barrier semaphores. Data moves between devices by JAX's collectives and lax.ppermute only.
A program may use at most 64 MiB of HBM per device.

```python
import math
import jax
import jax.numpy as jnp
from jax import lax

D = 8192
FF = 28672
Q = 32
R = 32
TOKENS = 12288


def apply_scales(key, base, top):
    key_rows, key_cols = jax.random.split(key, 2)
    row_count, col_count = base.shape
    row_scale = jnp.exp(jax.random.uniform(key_rows, (row_count, 1), jnp.float32) * math.log(top))
    col_scale = jnp.exp(jax.random.uniform(key_cols, (1, col_count), jnp.float32) * math.log(top))
    return base * row_scale * col_scale / (math.sqrt(col_count) * 0.5 * top)


def draw_query_left(key, part):
    key = jax.random.fold_in(key, 11)
    key_base, key_scale = jax.random.split(key)
    base = jnp.clip(jax.random.normal(key_base, (Q * R, FF), jnp.float32), -6.0, 6.0)
    return apply_scales(key_scale, base, 10.0).astype(jnp.bfloat16)


def draw_query_right(key, part):
    key = jax.random.fold_in(key, 23)
    key_base, key_scale = jax.random.split(key)
    base = jnp.clip(jax.random.normal(key_base, (Q * R, D), jnp.float32), -6.0, 6.0)
    return apply_scales(key_scale, base, 10.0).astype(jnp.bfloat16)


def level_of(key, extent, cuts, smallest, top_value):
    loudness = 1.0
    for dim, shards_of in cuts:
        draws = jax.random.uniform(jax.random.fold_in(jax.random.fold_in(key, 6), dim), (shards_of,), jnp.float32, smallest / len(cuts), top_value / len(cuts))
        loudness = loudness * jnp.repeat(jnp.exp(draws), extent[dim] // shards_of).reshape((-1,) + (1,) * (len(extent) - 1 - dim))
    return loudness


def noise(stream_key, shape, spread, reach, shards=(), dtype=jnp.bfloat16):
    array = spread * jax.random.normal(stream_key, shape, jnp.float32)
    if shards:
        array = array * level_of(stream_key, shape, shards, -0.22, 0.18)
    return jnp.clip(array, -reach, reach).astype(dtype)


def setup_inputs(seed: int = 0) -> dict:
    streams_of = jax.random.split(jax.random.key(seed), 5)
    return {
        "hidden_acts": noise(streams_of[0], (TOKENS, FF), 1.0, 6.0, ((0, 32), (1, 16))),
        "out_grads": noise(streams_of[1], (TOKENS, D), 1.0, 6.0, ((0, 32), (1, 16))),
        "query_left": draw_query_left(jax.random.fold_in(streams_of[4], 71), 0),
        "query_right": draw_query_right(jax.random.fold_in(streams_of[4], 71), 0),
    }


epsilon = 1e-06

def query_gram(panel, width):
    blocks = panel.astype(jnp.float32).reshape(Q, R, width)
    return jnp.einsum('qrf,qsf->qrs', blocks, blocks, precision=lax.Precision.HIGHEST)

def reference(hidden_acts, out_grads, query_left, query_right):
    proj_left = jnp.dot(hidden_acts, query_left.T, preferred_element_type=jnp.float32)
    proj_right = jnp.dot(out_grads, query_right.T, preferred_element_type=jnp.float32)
    gram_left = query_gram(query_left, FF)
    gram_right = query_gram(query_right, D)
    query_norm = jnp.sqrt(lax.optimization_barrier(jnp.sum(gram_left * gram_right, axis=(1, 2))) + epsilon)
    scores = lax.optimization_barrier(jnp.sum((proj_left * proj_right).reshape(TOKENS, Q, R), axis=2))
    return (scores / query_norm[None, :]).T
```

```python
import jax
import jax.numpy as jnp
from jax import lax
from jax.experimental import pallas as pl
from jax.experimental.pallas import tpu as pltpu
from jax.sharding import Mesh
from jax.sharding import PartitionSpec as P

R = 32
GROUP = 128

epsilon = 1e-06

NT = (((1,), (1,)), ((), ()))


def _project(q_ref, own_ref, other_ref, out_ref):
    n_own, n_other = own_ref.shape[0], other_ref.shape[0]
    q = q_ref[...]
    out_ref[:, :n_own] = lax.dot_general(q, own_ref[...], NT, preferred_element_type=jnp.float32)
    out_ref[:, n_own : n_own + n_other] = lax.dot_general(
        q, other_ref[...], NT, preferred_element_type=jnp.float32
    )
    out_ref[:, n_own + n_other :] = lax.dot_general(q, q, NT, preferred_element_type=jnp.float32)


def project(q, own, other):
    rows, k = q.shape
    tokens = own.shape[0] + other.shape[0]
    width = tokens + GROUP
    whole = lambda a: pl.BlockSpec(a.shape, lambda i: (0, 0))
    return pl.pallas_call(
        _project,
        grid=(rows // GROUP,),
        in_specs=[pl.BlockSpec((GROUP, k), lambda i: (i, 0)), whole(own), whole(other)],
        out_specs=pl.BlockSpec((GROUP, width), lambda i: (i, 0)),
        out_shape=jax.ShapeDtypeStruct((rows, width), jnp.float32),
        compiler_params=pltpu.CompilerParams(vmem_limit_bytes=40 * 2**20),
        cost_estimate=pl.CostEstimate(
            flops=2 * rows * k * width,
            bytes_accessed=2 * k * (rows + tokens) + 4 * rows * width,
            transcendentals=0,
        ),
    )(q, own, other)


def _finish(slot_ref, left_ref, right_ref, out_ref):
    left, right = left_ref[0], right_ref[0]
    for s in range(1, left_ref.shape[0]):
        left = left + left_ref[s]
        right = right + right_ref[s]
    both = jnp.sum(left * right, axis=0, keepdims=True)
    tokens = out_ref.shape[1]
    lanes = lax.broadcasted_iota(jnp.int32, (1, GROUP), 1)
    mine = lanes // R == slot_ref[0]
    square = jnp.sum(jnp.where(mine, both[:, tokens:], 0.0), axis=1, keepdims=True)
    out_ref[...] = both[:, :tokens] / jnp.sqrt(square + epsilon)


def finish(slot, left, right):
    tokens = left.shape[2] - GROUP
    return pl.pallas_call(
        _finish,
        in_specs=[
            pl.BlockSpec(memory_space=pltpu.SMEM),
            pl.BlockSpec(memory_space=pltpu.VMEM),
            pl.BlockSpec(memory_space=pltpu.VMEM),
        ],
        out_specs=pl.BlockSpec(memory_space=pltpu.VMEM),
        out_shape=jax.ShapeDtypeStruct((1, tokens), jnp.float32),
        compiler_params=pltpu.CompilerParams(vmem_limit_bytes=40 * 2**20),
        cost_estimate=pl.CostEstimate(
            flops=4 * left.size, bytes_accessed=8 * left.size, transcendentals=0
        ),
    )(slot, left, right)


def on_device(hidden_acts, out_grads, query_left, query_right):
    planes = lax.axis_size("z")
    owners = lax.axis_size(("x", "y"))
    tokens = hidden_acts.shape[0]
    swap = [(0, 1), (1, 0)]
    hidden_other = lax.ppermute(hidden_acts, "c", swap)
    grads_other = lax.ppermute(out_grads, "c", swap)
    left_rows = lax.all_gather(query_left, "z", axis=0, tiled=True)
    right_rows = lax.all_gather(query_right, "z", axis=0, tiled=True)

    def owned(rows, own, other):
        terms = project(rows, own, other)
        terms = terms.reshape(owners, terms.shape[0] // owners, terms.shape[1])
        return lax.all_to_all(terms, ("x", "y"), split_axis=0, concat_axis=0, tiled=True)

    right = owned(right_rows, out_grads, grads_other)
    left = owned(left_rows, hidden_acts, hidden_other)
    slot = lax.rem(lax.axis_index(("x", "y")), GROUP // R).astype(jnp.int32).reshape(1)
    scores = finish(slot, left, right)

    core = lax.axis_index("c")
    halves = scores.reshape(2, tokens)
    by_core = jnp.where(core == 0, halves, halves[::-1])
    sent = jnp.broadcast_to(by_core[:, None, :], (2, owners, tokens)).reshape(2 * owners, 1, tokens)
    got = lax.all_to_all(sent, ("c", "x", "y"), split_axis=0, concat_axis=0, tiled=True)
    return got.reshape(2, planes, tokens).transpose(1, 0, 2).reshape(2 * planes, tokens)


def solution(mesh):
    devices = mesh.devices
    planes = devices.shape[0] // 2
    owners = devices.shape[1]
    side = int(round(owners**0.5))
    grid = Mesh(devices.reshape(planes, 2, side, side), ("z", "c", "x", "y"))
    placed = P(("z", "c"), ("x", "y"))
    return jax.shard_map(
        on_device,
        mesh=grid,
        in_specs=(placed,) * 4,
        out_specs=P(None, ("z", "c")),
        check_vma=False,
    )
```

```python
import jax
import jax.numpy as jnp
from jax import lax
from jax.experimental import pallas as pl
from jax.experimental.pallas import tpu as pltpu
from jax.sharding import Mesh
from jax.sharding import PartitionSpec as P

R = 32
GROUP = 128
TOP = 2.0**15
POWERS = (64, 32, 16, 8, 4, 2, 1)

epsilon = 1e-06

NT = (((1,), (1,)), ((), ()))
VMEM = pl.BlockSpec(memory_space=pltpu.VMEM)
SMEM = pl.BlockSpec(memory_space=pltpu.SMEM)


def params():
    return pltpu.CompilerParams(vmem_limit_bytes=40 * 2**20)


def dot(a, b):
    return lax.dot_general(a, b, NT, preferred_element_type=jnp.float32)


def pack(left, right):
    rows, wide = left.shape
    narrow = right.shape[1]

    def scaled(x):
        x = x.astype(jnp.float32)
        largest = jnp.maximum(jnp.max(jnp.abs(x), axis=1, keepdims=True), 2.0**-100)
        scale, exponent = jnp.ones_like(largest), jnp.zeros_like(largest)
        for p in POWERS:
            more = largest * (scale * 2.0**p) < TOP
            scale = jnp.where(more, scale * 2.0**p, scale)
            exponent = jnp.where(more, exponent + p, exponent)
        return x * scale, exponent

    def body(left_ref, right_ref, out):
        left_rows, left_exponent = scaled(left_ref[...])
        right_rows, right_exponent = scaled(right_ref[...])
        out[:, :wide] = left_rows.astype(out.dtype)
        out[:, wide : wide + narrow] = right_rows.astype(out.dtype)
        lanes = lax.broadcasted_iota(jnp.int32, (rows, GROUP), 1)
        out[:, wide + narrow :] = jnp.where(lanes == 0, left_exponent, right_exponent).astype(out.dtype)

    return pl.pallas_call(
        body,
        in_specs=[VMEM] * 2,
        out_specs=VMEM,
        out_shape=jax.ShapeDtypeStruct((rows, wide + narrow + GROUP), left.dtype),
        compiler_params=params(),
    )(left, right)


def unscaled(rows, exponent):
    factor = jnp.ones_like(exponent)
    for p in POWERS:
        more = exponent >= p
        factor = jnp.where(more, factor * 2.0**-p, factor)
        exponent = jnp.where(more, exponent - p, exponent)
    return (rows.astype(jnp.float32) * factor).astype(rows.dtype)


def project(queries, hidden, hidden_other, grads, grads_other):
    rows = queries.shape[0]
    own, wide = hidden.shape
    narrow = grads.shape[1]
    width = 4 * own + GROUP

    def body(q_ref, h, ho, g, go, out):
        exponents = q_ref[:, wide + narrow :].astype(jnp.float32)
        left = unscaled(q_ref[:, :wide], exponents[:, 0:1])
        right = unscaled(q_ref[:, wide : wide + narrow], exponents[:, 1:2])
        out[:, :own] = dot(left, h[...])
        out[:, own : 2 * own] = dot(left, ho[...])
        out[:, 2 * own : 3 * own] = dot(right, g[...])
        out[:, 3 * own : 4 * own] = dot(right, go[...])
        query = lax.broadcasted_iota(jnp.int32, (GROUP, GROUP), 0) // R
        block = lax.broadcasted_iota(jnp.int32, (GROUP, GROUP), 1) // R
        next_right = jnp.concatenate([right[GROUP - R :], right[: GROUP - R]], axis=0)
        out[:, 4 * own :] = jnp.where(query == block, dot(left, left), dot(right, next_right))

    whole = lambda a: pl.BlockSpec(a.shape, lambda i: (0, 0))
    tokens = (hidden, hidden_other, grads, grads_other)
    return pl.pallas_call(
        body,
        grid=(rows // GROUP,),
        in_specs=[pl.BlockSpec((GROUP, queries.shape[1]), lambda i: (i, 0))]
        + [whole(a) for a in tokens],
        out_specs=pl.BlockSpec((GROUP, width), lambda i: (i, 0)),
        out_shape=jax.ShapeDtypeStruct((rows, width), jnp.float32),
        compiler_params=params(),
        cost_estimate=pl.CostEstimate(
            flops=rows * width * queries.shape[1],
            bytes_accessed=2 * (2 * own + rows) * queries.shape[1] + 4 * rows * width,
            transcendentals=0,
        ),
    )(queries, *tokens)


def finish(slot, terms):
    own = (terms.shape[2] - GROUP) // 4

    def body(slot_ref, terms_ref, out):
        total = terms_ref[0]
        for s in range(1, terms_ref.shape[0]):
            total = total + terms_ref[s]
        both = jnp.sum(total[:, : 2 * own] * total[:, 2 * own : 4 * own], axis=0, keepdims=True)
        gram = total[:, 4 * own :]
        gram = gram * pltpu.roll(gram, GROUP - R, 1)
        lanes = lax.broadcasted_iota(jnp.int32, (1, GROUP), 1)
        mine = lanes // R == slot_ref[0]
        square = jnp.sum(jnp.where(mine, gram, 0.0), axis=(0, 1), keepdims=True)
        out[...] = both / jnp.sqrt(square + epsilon)

    return pl.pallas_call(
        body,
        in_specs=[SMEM, VMEM],
        out_specs=VMEM,
        out_shape=jax.ShapeDtypeStruct((1, 2 * own), jnp.float32),
        compiler_params=params(),
    )(slot, terms)


def on_device(hidden_acts, out_grads, query_left, query_right):
    planes = lax.axis_size("z")
    owners = lax.axis_size(("x", "y"))
    tokens = hidden_acts.shape[0]
    swap = [(0, 1), (1, 0)]
    hidden_other = lax.ppermute(hidden_acts, "c", swap)
    grads_other = lax.ppermute(out_grads, "c", swap)

    sent = pack(query_left, query_right).astype(jnp.float16)
    queries = lax.all_gather(sent, "z", axis=0, tiled=True).astype(query_left.dtype)
    terms = project(queries, hidden_acts, hidden_other, out_grads, grads_other)
    terms = terms.reshape(owners, terms.shape[0] // owners, terms.shape[1])
    terms = lax.all_to_all(terms, ("x", "y"), split_axis=0, concat_axis=0, tiled=True)
    slot = lax.rem(lax.axis_index(("x", "y")), GROUP // R).astype(jnp.int32).reshape(1)
    scores = finish(slot, terms)

    halves = scores.reshape(2, tokens)
    by_core = jnp.where(lax.axis_index("c") == 0, halves, halves[::-1])
    sent = jnp.broadcast_to(by_core[:, None, :], (2, owners, tokens)).reshape(2 * owners, 1, tokens)
    got = lax.all_to_all(sent, ("c", "x", "y"), split_axis=0, concat_axis=0, tiled=True)
    return got.reshape(2, planes, tokens).transpose(1, 0, 2).reshape(2 * planes, tokens)


def solution(mesh):
    devices = mesh.devices
    planes = devices.shape[0] // 2
    owners = devices.shape[1]
    side = int(round(owners**0.5))
    grid = Mesh(devices.reshape(planes, 2, side, side), ("z", "c", "x", "y"))
    placed = P(("z", "c"), ("x", "y"))
    return jax.shard_map(
        on_device,
        mesh=grid,
        in_specs=(placed,) * 4,
        out_specs=P(None, ("z", "c")),
        check_vma=False,
    )
```

```python
import jax
import jax.numpy as jnp
from jax import lax
from jax.experimental import pallas as pl
from jax.experimental.pallas import tpu as pltpu
from jax.sharding import Mesh
from jax.sharding import PartitionSpec as P

R = 32
GROUP = 128
CLASSES = 2
TOP = 2.0**15
POWERS = (64, 32, 16, 8, 4, 2, 1)
WEIGHTS = (20, 0.01)

epsilon = 1e-06

NT = (((1,), (1,)), ((), ()))
VMEM = pl.BlockSpec(memory_space=pltpu.VMEM)
SMEM = pl.BlockSpec(memory_space=pltpu.SMEM)


def params():
    return pltpu.CompilerParams(vmem_limit_bytes=16 * 2**20)


def dot(a, b):
    return lax.dot_general(a, b, NT, preferred_element_type=jnp.float32)


def pack(left, right):
    rows, wide = left.shape
    narrow = right.shape[1]

    def scaled(x):
        x = x.astype(jnp.float32)
        largest = jnp.maximum(jnp.max(jnp.abs(x), axis=1, keepdims=True), 2.0**-100)
        scale, exponent = jnp.ones_like(largest), jnp.zeros_like(largest)
        for p in POWERS:
            more = largest * (scale * 2.0**p) < TOP
            scale = jnp.where(more, scale * 2.0**p, scale)
            exponent = jnp.where(more, exponent + p, exponent)
        return x * scale, exponent

    def body(left_ref, right_ref, out):
        left_rows, left_exponent = scaled(left_ref[...])
        right_rows, right_exponent = scaled(right_ref[...])
        out[:, :wide] = left_rows.astype(out.dtype)
        out[:, wide : wide + narrow] = right_rows.astype(out.dtype)
        lanes = lax.broadcasted_iota(jnp.int32, (rows, GROUP), 1)
        out[:, wide + narrow :] = jnp.where(lanes == 0, left_exponent, right_exponent).astype(out.dtype)

    return pl.pallas_call(
        body,
        in_specs=[VMEM] * 2,
        out_specs=VMEM,
        out_shape=jax.ShapeDtypeStruct((rows, wide + narrow + GROUP), left.dtype),
        compiler_params=params(),
    )(left, right)


def unscaled(rows, exponent):
    factor = jnp.ones_like(exponent)
    for p in POWERS:
        more = exponent >= p
        factor = jnp.where(more, factor * 2.0**-p, factor)
        exponent = jnp.where(more, exponent - p, exponent)
    return (rows.astype(jnp.float32) * factor).astype(rows.dtype)


def project(weight, pieces, hidden, hidden_other, grads, grads_other):
    rows = sum(p.shape[0] for p in pieces)
    packed = pieces[0].shape[1]
    own, wide = hidden.shape
    narrow = grads.shape[1]
    width = 4 * own + GROUP

    def body(*refs):
        q_refs, (h, ho, g, go, out) = refs[: len(pieces)], refs[len(pieces) :]
        blocks = [(q, at) for q in q_refs for at in range(0, q.shape[0], GROUP)]
        query = lax.broadcasted_iota(jnp.int32, (GROUP, GROUP), 0) // R
        block = lax.broadcasted_iota(jnp.int32, (GROUP, GROUP), 1) // R
        for i, (q_ref, at) in enumerate(blocks):
            here, there = slice(at, at + GROUP), slice(i * GROUP, (i + 1) * GROUP)
            exponents = q_ref[here, wide + narrow :].astype(jnp.float32)
            left = unscaled(q_ref[here, :wide], exponents[:, 0:1])
            right = unscaled(q_ref[here, wide : wide + narrow], exponents[:, 1:2])
            out[there, :own] = dot(left, h[...])
            out[there, own : 2 * own] = dot(left, ho[...])
            out[there, 2 * own : 3 * own] = dot(right, g[...])
            out[there, 3 * own : 4 * own] = dot(right, go[...])
            next_right = jnp.concatenate([right[GROUP - R :], right[: GROUP - R]], axis=0)
            out[there, 4 * own :] = jnp.where(query == block, dot(left, left), dot(right, next_right))

    return pl.pallas_call(
        body,
        in_specs=[VMEM] * (len(pieces) + 4),
        out_specs=VMEM,
        out_shape=jax.ShapeDtypeStruct((rows, width), jnp.float32),
        compiler_params=params(),
        cost_estimate=pl.CostEstimate(
            flops=int(weight * rows * width * packed),
            bytes_accessed=int(weight * 2 * rows * packed),
            transcendentals=0,
        ),
    )(*pieces, hidden, hidden_other, grads, grads_other)


def finish(place, parts):
    owners = parts[0].shape[0]
    own = (parts[0].shape[2] - GROUP) // 4

    def body(place_ref, *refs):
        out = refs[-1]
        core, parity, slot = place_ref[0], place_ref[1], place_ref[2]
        lanes = lax.broadcasted_iota(jnp.int32, (1, GROUP), 1)
        at = lax.broadcasted_iota(jnp.int32, (CLASSES, own + GROUP), 0)
        mine = jnp.zeros((CLASSES, own + GROUP), jnp.float32)
        theirs = mine
        for k, ref in enumerate(refs[:-1]):
            total = ref[0]
            for s in range(1, owners):
                total = total + ref[s]
            both = jnp.sum(total[:, : 2 * own] * total[:, 2 * own : 4 * own], axis=0, keepdims=True)
            gram = total[:, 4 * own :]
            gram = gram * pltpu.roll(gram, GROUP - R, 1)
            square = jnp.sum(jnp.where(lanes // R == slot, gram, 0.0), axis=(0, 1), keepdims=True)
            square = jnp.broadcast_to(square, (1, GROUP))
            row = at == lax.rem(parity + k, CLASSES)
            mine = jnp.where(row, jnp.concatenate([both[:, :own], square], 1), mine)
            theirs = jnp.where(row, jnp.concatenate([both[:, own:], square], 1), theirs)
        first = jnp.where(core == 0, mine, theirs)
        second = jnp.where(core == 0, theirs, mine)
        out[:owners] = jnp.broadcast_to(first[None], (owners, *first.shape))
        out[owners:] = jnp.broadcast_to(second[None], (owners, *second.shape))

    return pl.pallas_call(
        body,
        in_specs=[SMEM] + [VMEM] * len(parts),
        out_specs=VMEM,
        out_shape=jax.ShapeDtypeStruct((2 * owners, CLASSES, own + GROUP), jnp.float32),
        compiler_params=params(),
    )(place, *parts)


def scores_of(got, shares):
    own = got.shape[2] - GROUP
    queries = got.shape[0] // 2 // shares

    def body(got_ref, out):
        for core in range(2):
            for a in range(queries):
                first = (core * queries + a) * shares
                total = got_ref[first]
                for b in range(1, shares):
                    total = total + got_ref[first + b]
                values = total[:, :own] / jnp.sqrt(total[:, own : own + 1] + epsilon)
                for g in range(CLASSES):
                    row = 2 * (CLASSES * a + g) + core
                    out[row : row + 1, :] = values[g : g + 1]

    return pl.pallas_call(
        body,
        in_specs=[VMEM],
        out_specs=VMEM,
        out_shape=jax.ShapeDtypeStruct((2 * CLASSES * queries, own), jnp.float32),
        compiler_params=params(),
    )(got)


def on_device(hidden_acts, out_grads, query_left, query_right):
    planes = lax.axis_size(("zh", "zp"))
    owners = lax.axis_size(("x", "y"))

    def from_plane(block, ahead):
        pairs = [((z + ahead) % planes, z) for z in range(planes)]
        return lax.ppermute(block, ("zh", "zp"), pairs)

    swap = [(0, 1), (1, 0)]
    hidden_other = lax.ppermute(hidden_acts, "c", swap)
    grads_other = lax.ppermute(out_grads, "c", swap)
    tokens = (hidden_acts, hidden_other, out_grads, grads_other)

    sent = pack(query_left, query_right).astype(jnp.float16)
    here = lax.all_gather(sent, "zh", axis=0, tiled=True).astype(query_left.dtype)
    half = here.shape[0] // 2
    there = (from_plane(here[:half], 1), from_plane(here[half:], -1))

    def owned(terms):
        terms = terms.reshape(owners, terms.shape[0] // owners, terms.shape[1])
        return lax.all_to_all(terms, ("x", "y"), split_axis=0, concat_axis=0, tiled=True)

    first_terms = project(WEIGHTS[0], (here,), *tokens)
    first = owned(first_terms)
    there, _ = lax.optimization_barrier((there, first_terms))
    second_terms, first = lax.optimization_barrier((project(WEIGHTS[1], there, *tokens), first))
    second = owned(second_terms)

    share = here.shape[0] // owners
    shares = R // share
    place = jnp.stack(
        [
            lax.axis_index("c"),
            lax.axis_index("zp"),
            lax.rem(lax.axis_index(("x", "y")) // shares, GROUP // R),
        ]
    ).astype(jnp.int32)
    sums = finish(place, (first, second))
    got = lax.all_to_all(sums, ("c", "x", "y"), split_axis=0, concat_axis=0, tiled=True)
    return scores_of(got, shares)


def solution(mesh):
    devices = mesh.devices
    planes = devices.shape[0] // 2
    owners = devices.shape[1]
    side = int(round(owners**0.5))
    shape = (planes // CLASSES, CLASSES, 2, side, side)
    grid = Mesh(devices.reshape(shape), ("zh", "zp", "c", "x", "y"))
    placed = P(("zh", "zp", "c"), ("x", "y"))
    return jax.shard_map(
        on_device,
        mesh=grid,
        in_specs=(placed,) * 4,
        out_specs=P(None, ("zh", "zp", "c")),
        check_vma=False,
    )
```

```python
import jax
import jax.numpy as jnp
from jax import lax
from jax.experimental import pallas as pl
from jax.experimental.pallas import tpu as pltpu
from jax.sharding import Mesh
from jax.sharding import PartitionSpec as P

R = 32
GROUP = 128
CLASSES = 2
TOP = 2.0**15
POWERS = (64, 32, 16, 8, 4, 2, 1)
WEIGHTS = (20, 0.01)

epsilon = 1e-06

NT = (((1,), (1,)), ((), ()))
VMEM = pl.BlockSpec(memory_space=pltpu.VMEM)
SMEM = pl.BlockSpec(memory_space=pltpu.SMEM)


def params():
    return pltpu.CompilerParams(vmem_limit_bytes=16 * 2**20)


def dot(a, b):
    return lax.dot_general(a, b, NT, preferred_element_type=jnp.float32)


def pack(left, right):
    rows, wide = left.shape
    narrow = right.shape[1]

    def scaled(x):
        x = x.astype(jnp.float32)
        largest = jnp.maximum(jnp.max(jnp.abs(x), axis=1, keepdims=True), 2.0**-100)
        scale, exponent = jnp.ones_like(largest), jnp.zeros_like(largest)
        for p in POWERS:
            more = largest * (scale * 2.0**p) < TOP
            scale = jnp.where(more, scale * 2.0**p, scale)
            exponent = jnp.where(more, exponent + p, exponent)
        return x * scale, exponent

    def body(left_ref, right_ref, out):
        left_rows, left_exponent = scaled(left_ref[...])
        right_rows, right_exponent = scaled(right_ref[...])
        out[:, :wide] = left_rows.astype(out.dtype)
        out[:, wide : wide + narrow] = right_rows.astype(out.dtype)
        lanes = lax.broadcasted_iota(jnp.int32, (rows, GROUP), 1)
        out[:, wide + narrow :] = jnp.where(lanes == 0, left_exponent, right_exponent).astype(out.dtype)

    return pl.pallas_call(
        body,
        in_specs=[VMEM] * 2,
        out_specs=VMEM,
        out_shape=jax.ShapeDtypeStruct((rows, wide + narrow + GROUP), left.dtype),
        compiler_params=params(),
    )(left, right)


def unscaled(rows, exponent):
    factor = jnp.ones_like(exponent)
    for p in POWERS:
        more = exponent >= p
        factor = jnp.where(more, factor * 2.0**-p, factor)
        exponent = jnp.where(more, exponent - p, exponent)
    return (rows.astype(jnp.float32) * factor).astype(rows.dtype)


def project(weight, wide, pieces, mine, theirs):
    rows = sum(p.shape[0] for p in pieces)
    packed = pieces[0].shape[1]
    own, both = mine.shape
    width = 4 * own + GROUP

    def body(*refs):
        q_refs, (mine_ref, theirs_ref, out, left, right) = refs[: len(pieces)], refs[len(pieces) :]
        at = 0
        for q_ref in q_refs:
            here = slice(at, at + q_ref.shape[0])
            exponents = q_ref[:, both:].astype(jnp.float32)
            left[here] = unscaled(q_ref[:, :wide], exponents[:, 0:1])
            right[here] = unscaled(q_ref[:, wide:both], exponents[:, 1:2])
            at += q_ref.shape[0]
        out[:, :own] = dot(left[...], mine_ref[:, :wide])
        out[:, own : 2 * own] = dot(left[...], theirs_ref[:, :wide])
        out[:, 2 * own : 3 * own] = dot(right[...], mine_ref[:, wide:])
        out[:, 3 * own : 4 * own] = dot(right[...], theirs_ref[:, wide:])
        query = lax.broadcasted_iota(jnp.int32, (GROUP, GROUP), 0) // R
        block = lax.broadcasted_iota(jnp.int32, (GROUP, GROUP), 1) // R
        for at in range(0, rows, GROUP):
            here = slice(at, at + GROUP)
            x, y = left[here], right[here]
            next_y = jnp.concatenate([y[GROUP - R :], y[: GROUP - R]], axis=0)
            out[here, 4 * own :] = jnp.where(query == block, dot(x, x), dot(y, next_y))

    return pl.pallas_call(
        body,
        in_specs=[VMEM] * (len(pieces) + 2),
        out_specs=VMEM,
        out_shape=jax.ShapeDtypeStruct((rows, width), jnp.float32),
        scratch_shapes=[
            pltpu.VMEM((rows, wide), mine.dtype),
            pltpu.VMEM((rows, both - wide), mine.dtype),
        ],
        compiler_params=params(),
        cost_estimate=pl.CostEstimate(
            flops=int(weight * rows * width * packed),
            bytes_accessed=int(weight * 2 * rows * packed),
            transcendentals=0,
        ),
    )(*pieces, mine, theirs)


def finish(place, parts):
    owners = parts[0].shape[0]
    own = (parts[0].shape[2] - GROUP) // 4

    def body(place_ref, *refs):
        out = refs[-1]
        core, parity, slot = place_ref[0], place_ref[1], place_ref[2]
        lanes = lax.broadcasted_iota(jnp.int32, (1, GROUP), 1)
        at = lax.broadcasted_iota(jnp.int32, (CLASSES, own + GROUP), 0)
        mine = jnp.zeros((CLASSES, own + GROUP), jnp.float32)
        theirs = mine
        for k, ref in enumerate(refs[:-1]):
            total = ref[0]
            for s in range(1, owners):
                total = total + ref[s]
            both = jnp.sum(total[:, : 2 * own] * total[:, 2 * own : 4 * own], axis=0, keepdims=True)
            gram = total[:, 4 * own :]
            gram = gram * pltpu.roll(gram, GROUP - R, 1)
            square = jnp.sum(jnp.where(lanes // R == slot, gram, 0.0), axis=(0, 1), keepdims=True)
            square = jnp.broadcast_to(square, (1, GROUP))
            row = at == lax.rem(parity + k, CLASSES)
            mine = jnp.where(row, jnp.concatenate([both[:, :own], square], 1), mine)
            theirs = jnp.where(row, jnp.concatenate([both[:, own:], square], 1), theirs)
        first = jnp.where(core == 0, mine, theirs)
        second = jnp.where(core == 0, theirs, mine)
        out[:owners] = jnp.broadcast_to(first[None], (owners, *first.shape))
        out[owners:] = jnp.broadcast_to(second[None], (owners, *second.shape))

    return pl.pallas_call(
        body,
        in_specs=[SMEM] + [VMEM] * len(parts),
        out_specs=VMEM,
        out_shape=jax.ShapeDtypeStruct((2 * owners, CLASSES, own + GROUP), jnp.float32),
        compiler_params=params(),
    )(place, *parts)


def scores_of(got, shares):
    own = got.shape[2] - GROUP
    queries = got.shape[0] // 2 // shares

    def body(got_ref, out):
        for core in range(2):
            for a in range(queries):
                first = (core * queries + a) * shares
                total = got_ref[first]
                for b in range(1, shares):
                    total = total + got_ref[first + b]
                values = total[:, :own] / jnp.sqrt(total[:, own : own + 1] + epsilon)
                for g in range(CLASSES):
                    row = 2 * (CLASSES * a + g) + core
                    out[row : row + 1, :] = values[g : g + 1]

    return pl.pallas_call(
        body,
        in_specs=[VMEM],
        out_specs=VMEM,
        out_shape=jax.ShapeDtypeStruct((2 * CLASSES * queries, own), jnp.float32),
        compiler_params=params(),
    )(got)


def on_device(hidden_acts, out_grads, query_left, query_right):
    planes = lax.axis_size(("zh", "zp"))
    owners = lax.axis_size(("x", "y"))

    def from_plane(block, ahead):
        pairs = [((z + ahead) % planes, z) for z in range(planes)]
        return lax.ppermute(block, ("zh", "zp"), pairs)

    mine = jnp.concatenate([hidden_acts, out_grads], axis=1)
    tokens = (mine, lax.ppermute(mine, "c", [(0, 1), (1, 0)]))
    wide = hidden_acts.shape[1]

    sent = pack(query_left, query_right).astype(jnp.float16)
    here = lax.all_gather(sent, "zh", axis=0, tiled=True)
    half = here.shape[0] // 2
    here = (here[:half].astype(query_left.dtype), here[half:].astype(query_left.dtype))
    there = (from_plane(here[0], 1), from_plane(here[1], -1))

    def owned(terms):
        terms = terms.reshape(owners, terms.shape[0] // owners, terms.shape[1])
        return lax.all_to_all(terms, ("x", "y"), split_axis=0, concat_axis=0, tiled=True)

    first_terms = project(WEIGHTS[0], wide, here, *tokens)
    first = owned(first_terms)
    there, _ = lax.optimization_barrier((there, first_terms))
    second_terms, first = lax.optimization_barrier((project(WEIGHTS[1], wide, there, *tokens), first))
    second = owned(second_terms)

    share = 2 * half // owners
    shares = R // share
    place = jnp.stack(
        [
            lax.axis_index("c"),
            lax.axis_index("zp"),
            lax.rem(lax.axis_index(("x", "y")) // shares, GROUP // R),
        ]
    ).astype(jnp.int32)
    sums = finish(place, (first, second))
    got = lax.all_to_all(sums, ("c", "x", "y"), split_axis=0, concat_axis=0, tiled=True)
    return scores_of(got, shares)


def solution(mesh):
    devices = mesh.devices
    planes = devices.shape[0] // 2
    owners = devices.shape[1]
    side = int(round(owners**0.5))
    shape = (planes // CLASSES, CLASSES, 2, side, side)
    grid = Mesh(devices.reshape(shape), ("zh", "zp", "c", "x", "y"))
    placed = P(("zh", "zp", "c"), ("x", "y"))
    return jax.shard_map(
        on_device,
        mesh=grid,
        in_specs=(placed,) * 4,
        out_specs=P(None, ("zh", "zp", "c")),
        check_vma=False,
    )
```

```python
import jax
import jax.numpy as jnp
from jax import lax
from jax.experimental import pallas as pl
from jax.experimental.pallas import tpu as pltpu
from jax.sharding import Mesh
from jax.sharding import PartitionSpec as P

R = 32
GROUP = 128
OWNERS = 16
CLASSES = 2
TOP = 2.0**15
POWERS = (64, 32, 16, 8, 4, 2, 1)
WEIGHTS = (1, 0.01)

epsilon = 1e-06

NT = (((1,), (1,)), ((), ()))
VMEM = pl.BlockSpec(memory_space=pltpu.VMEM)
SMEM = pl.BlockSpec(memory_space=pltpu.SMEM)


def params():
    return pltpu.CompilerParams(vmem_limit_bytes=16 * 2**20)


def dot(a, b):
    return lax.dot_general(a, b, NT, preferred_element_type=jnp.float32)


def pack(left, right):
    rows, wide = left.shape
    narrow = right.shape[1]

    def scaled(x):
        x = x.astype(jnp.float32)
        largest = jnp.maximum(jnp.max(jnp.abs(x), axis=1, keepdims=True), 2.0**-100)
        scale, exponent = jnp.ones_like(largest), jnp.zeros_like(largest)
        for p in POWERS:
            more = largest * (scale * 2.0**p) < TOP
            scale = jnp.where(more, scale * 2.0**p, scale)
            exponent = jnp.where(more, exponent + p, exponent)
        return x * scale, exponent

    def body(left_ref, right_ref, out):
        left_rows, left_exponent = scaled(left_ref[...])
        right_rows, right_exponent = scaled(right_ref[...])
        out[:, :wide] = left_rows.astype(out.dtype)
        out[:, wide : wide + narrow] = right_rows.astype(out.dtype)
        lanes = lax.broadcasted_iota(jnp.int32, (rows, GROUP), 1)
        out[:, wide + narrow :] = jnp.where(lanes == 0, left_exponent, right_exponent).astype(out.dtype)

    return pl.pallas_call(
        body,
        in_specs=[VMEM] * 2,
        out_specs=VMEM,
        out_shape=jax.ShapeDtypeStruct((rows, wide + narrow + GROUP), left.dtype),
        compiler_params=params(),
    )(left, right)


def unscaled(rows, exponent):
    factor = jnp.ones_like(exponent)
    for p in POWERS:
        more = exponent >= p
        factor = jnp.where(more, factor * 2.0**-p, factor)
        exponent = jnp.where(more, exponent - p, exponent)
    return (rows.astype(jnp.float32) * factor).astype(rows.dtype)


def project(weight, wide, pieces, mine, theirs):
    rows = sum(p.shape[0] for p in pieces)
    packed = pieces[0].shape[1]
    own, both = mine.shape
    half = 4 * own
    width = 2 * half + GROUP
    share = rows // OWNERS

    def body(*refs):
        q_refs, (mine_ref, theirs_ref, out, left, right) = refs[: len(pieces)], refs[len(pieces) :]
        at = 0
        for q_ref in q_refs:
            here = slice(at, at + q_ref.shape[0])
            exponents = q_ref[:, both:].astype(jnp.float32)
            left[here] = unscaled(q_ref[:, :wide], exponents[:, 0:1])
            right[here] = unscaled(q_ref[:, wide:both], exponents[:, 1:2])
            at += q_ref.shape[0]
        for at, factors, tokens in (
            (0, left, mine_ref[:, :wide]),
            (own, left, theirs_ref[:, :wide]),
            (2 * own, right, mine_ref[:, wide:]),
            (3 * own, right, theirs_ref[:, wide:]),
        ):
            value = dot(factors[...], tokens).reshape(OWNERS, share, own)
            out[:, :, at : at + own] = value[:, : share // 2]
            out[:, :, half + at : half + at + own] = value[:, share // 2 :]
        query = lax.broadcasted_iota(jnp.int32, (GROUP, GROUP), 0) // R
        block = lax.broadcasted_iota(jnp.int32, (GROUP, GROUP), 1) // R
        count = GROUP // share
        shape = (count, share // 2, GROUP)
        first = lax.broadcasted_iota(jnp.int32, shape, 0) * share // R
        ahead = lax.rem(lax.broadcasted_iota(jnp.int32, shape, 2) // R - first + GROUP // R, GROUP // R)
        for i in range(rows // GROUP):
            here = slice(i * GROUP, (i + 1) * GROUP)
            x, y = left[here], right[here]
            next_y = jnp.concatenate([y[GROUP - R :], y[: GROUP - R]], axis=0)
            gram = jnp.where(query == block, dot(x, x), dot(y, next_y))
            moved = pltpu.roll(gram, 2 * R, 1).reshape(count, share, GROUP)
            gram = gram.reshape(count, share, GROUP)
            out[i * count : (i + 1) * count, :, 2 * half :] = jnp.where(
                ahead < 2, gram[:, : share // 2], moved[:, share // 2 :]
            )

    return pl.pallas_call(
        body,
        in_specs=[VMEM] * (len(pieces) + 2),
        out_specs=VMEM,
        out_shape=jax.ShapeDtypeStruct((OWNERS, share // 2, width), jnp.float32),
        scratch_shapes=[
            pltpu.VMEM((rows, wide), mine.dtype),
            pltpu.VMEM((rows, both - wide), mine.dtype),
        ],
        compiler_params=params(),
        cost_estimate=pl.CostEstimate(
            flops=int(weight * rows * half * packed),
            bytes_accessed=int(weight * 2 * rows * packed),
            transcendentals=0,
        ),
    )(*pieces, mine, theirs)


def class_rows(place, terms):
    half = (terms.shape[2] - GROUP) // 2
    own = half // 4
    total = terms[0]
    for s in range(1, OWNERS):
        total = total + terms[s]
    products = total[:, : 2 * own] * total[:, 2 * own : half]
    products += total[:, half : half + 2 * own] * total[:, half + 2 * own : 2 * half]
    both = jnp.sum(products, axis=0, keepdims=True)
    gram = total[:, 2 * half :]
    gram = gram * pltpu.roll(gram, GROUP - R, 1)
    lanes = lax.broadcasted_iota(jnp.int32, (1, GROUP), 1)
    lefts = lax.rem(lanes // R + place[2], 2) == 0
    square = jnp.sum(jnp.where(lefts, gram, 0.0), axis=(0, 1), keepdims=True)
    square = jnp.broadcast_to(square, (1, GROUP))
    mine = jnp.concatenate([both[:, :own], square], axis=1)
    theirs = jnp.concatenate([both[:, own:], square], axis=1)
    return jnp.where(place[0] == 0, mine, theirs), jnp.where(place[0] == 0, theirs, mine)


def finish_first(place, terms):
    width = (terms.shape[2] - GROUP) // 8 + GROUP

    def body(place_ref, terms_ref, out):
        out[0:1], out[1:2] = class_rows(place_ref, terms_ref)

    return pl.pallas_call(
        body,
        in_specs=[SMEM, VMEM],
        out_specs=VMEM,
        out_shape=jax.ShapeDtypeStruct((2, width), jnp.float32),
        compiler_params=params(),
        cost_estimate=pl.CostEstimate(
            flops=10_000_000_000, bytes_accessed=4 * terms.size, transcendentals=0
        ),
    )(place, terms)


def finish(place, first_rows, terms):
    width = first_rows.shape[1]

    def body(place_ref, first_ref, terms_ref, out):
        second = class_rows(place_ref, terms_ref)
        at = lax.broadcasted_iota(jnp.int32, (CLASSES, width), 0)
        for core in range(2):
            rows = jnp.where(at == place_ref[1], first_ref[core : core + 1], second[core])
            out[core * OWNERS : (core + 1) * OWNERS] = jnp.broadcast_to(
                rows[None], (OWNERS, CLASSES, width)
            )

    return pl.pallas_call(
        body,
        in_specs=[SMEM, VMEM, VMEM],
        out_specs=VMEM,
        out_shape=jax.ShapeDtypeStruct((2 * OWNERS, CLASSES, width), jnp.float32),
        compiler_params=params(),
    )(place, first_rows, terms)


def scores_of(got, shares):
    own = got.shape[2] - GROUP
    queries = got.shape[0] // 2 // shares

    def body(got_ref, out):
        for core in range(2):
            for a in range(queries):
                first = (core * queries + a) * shares
                total = got_ref[first]
                for b in range(1, shares):
                    total = total + got_ref[first + b]
                values = total[:, :own] / jnp.sqrt(total[:, own : own + 1] + epsilon)
                for g in range(CLASSES):
                    row = 2 * (CLASSES * a + g) + core
                    out[row : row + 1, :] = values[g : g + 1]

    return pl.pallas_call(
        body,
        in_specs=[VMEM],
        out_specs=VMEM,
        out_shape=jax.ShapeDtypeStruct((2 * CLASSES * queries, own), jnp.float32),
        compiler_params=params(),
    )(got)


def on_device(hidden_acts, out_grads, query_left, query_right):
    planes = lax.axis_size(("zh", "zp"))

    def from_plane(block, ahead):
        pairs = [((z + ahead) % planes, z) for z in range(planes)]
        return lax.ppermute(block, ("zh", "zp"), pairs)

    mine = jnp.concatenate([hidden_acts, out_grads], axis=1)
    tokens = (mine, lax.ppermute(mine, "c", [(0, 1), (1, 0)]))
    wide = hidden_acts.shape[1]

    sent = pack(query_left, query_right).astype(jnp.float16)
    here = lax.all_gather(sent, "zh", axis=0, tiled=True)
    half = here.shape[0] // 2
    here = (here[:half].astype(query_left.dtype), here[half:].astype(query_left.dtype))
    there = (from_plane(here[0], 1), from_plane(here[1], -1))

    def owned(terms):
        return lax.all_to_all(terms, ("x", "y"), split_axis=0, concat_axis=0, tiled=True)

    share = 2 * half // OWNERS
    shares = R // share
    place = jnp.stack(
        [
            lax.axis_index("c"),
            lax.axis_index("zp"),
            lax.rem(lax.axis_index(("x", "y")) // shares, GROUP // R),
        ]
    ).astype(jnp.int32)

    first_terms = project(WEIGHTS[0], wide, here, *tokens)
    first = owned(first_terms)
    there, _ = lax.optimization_barrier((there, first_terms))
    second_terms, first = lax.optimization_barrier((project(WEIGHTS[1], wide, there, *tokens), first))
    second = owned(second_terms)
    sums = finish(place, finish_first(place, first), second)
    got = lax.all_to_all(sums, ("c", "x", "y"), split_axis=0, concat_axis=0, tiled=True)
    return scores_of(got, shares)


def solution(mesh):
    devices = mesh.devices
    planes = devices.shape[0] // 2
    owners = devices.shape[1]
    side = int(round(owners**0.5))
    shape = (planes // CLASSES, CLASSES, 2, side, side)
    grid = Mesh(devices.reshape(shape), ("zh", "zp", "c", "x", "y"))
    placed = P(("zh", "zp", "c"), ("x", "y"))
    return jax.shard_map(
        on_device,
        mesh=grid,
        in_specs=(placed,) * 4,
        out_specs=P(None, ("zh", "zp", "c")),
        check_vma=False,
    )
```

```python
import jax
import jax.numpy as jnp
from jax import lax
from jax.experimental import pallas as pl
from jax.experimental.pallas import tpu as pltpu
from jax.sharding import Mesh
from jax.sharding import PartitionSpec as P

R = 32
GROUP = 128
OWNERS = 16
CLASSES = 2
TOP = 2.0**15
POWERS = (64, 32, 16, 8, 4, 2, 1)
WEIGHTS = (20, 0.01)

epsilon = 1e-06

NT = (((1,), (1,)), ((), ()))
VMEM = pl.BlockSpec(memory_space=pltpu.VMEM)
SMEM = pl.BlockSpec(memory_space=pltpu.SMEM)


def params():
    return pltpu.CompilerParams(vmem_limit_bytes=16 * 2**20)


def dot(a, b):
    return lax.dot_general(a, b, NT, preferred_element_type=jnp.float32)


def pack(left, right):
    rows, wide = left.shape
    narrow = right.shape[1]

    def scaled(x):
        x = x.astype(jnp.float32)
        largest = jnp.maximum(jnp.max(jnp.abs(x), axis=1, keepdims=True), 2.0**-100)
        scale, exponent = jnp.ones_like(largest), jnp.zeros_like(largest)
        for p in POWERS:
            more = largest * (scale * 2.0**p) < TOP
            scale = jnp.where(more, scale * 2.0**p, scale)
            exponent = jnp.where(more, exponent + p, exponent)
        return x * scale, exponent

    def body(left_ref, right_ref, out):
        left_rows, left_exponent = scaled(left_ref[...])
        right_rows, right_exponent = scaled(right_ref[...])
        out[:, :wide] = left_rows.astype(out.dtype)
        out[:, wide : wide + narrow] = right_rows.astype(out.dtype)
        lanes = lax.broadcasted_iota(jnp.int32, (rows, GROUP), 1)
        out[:, wide + narrow :] = jnp.where(lanes == 0, left_exponent, right_exponent).astype(out.dtype)

    return pl.pallas_call(
        body,
        in_specs=[VMEM] * 2,
        out_specs=VMEM,
        out_shape=jax.ShapeDtypeStruct((rows, wide + narrow + GROUP), left.dtype),
        compiler_params=params(),
    )(left, right)


def unscaled(rows, exponent):
    factor = jnp.ones_like(exponent)
    for p in POWERS:
        more = exponent >= p
        factor = jnp.where(more, factor * 2.0**-p, factor)
        exponent = jnp.where(more, exponent - p, exponent)
    return (rows.astype(jnp.float32) * factor).astype(rows.dtype)


def project(weight, wide, pieces, mine, theirs):
    rows = sum(p.shape[0] for p in pieces)
    packed = pieces[0].shape[1]
    own, both = mine.shape
    half = 4 * own
    width = 2 * half + GROUP
    share = rows // OWNERS

    def body(*refs):
        q_refs, (mine_ref, theirs_ref, out, left, right) = refs[: len(pieces)], refs[len(pieces) :]
        at = 0
        for q_ref in q_refs:
            here = slice(at, at + q_ref.shape[0])
            exponents = q_ref[:, both:].astype(jnp.float32)
            left[here] = unscaled(q_ref[:, :wide], exponents[:, 0:1])
            right[here] = unscaled(q_ref[:, wide:both], exponents[:, 1:2])
            at += q_ref.shape[0]
        for at, factors, tokens in (
            (0, left, mine_ref[:, :wide]),
            (own, left, theirs_ref[:, :wide]),
            (2 * own, right, mine_ref[:, wide:]),
            (3 * own, right, theirs_ref[:, wide:]),
        ):
            value = dot(factors[...], tokens).reshape(OWNERS, share, own)
            out[:, :, at : at + own] = value[:, : share // 2]
            out[:, :, half + at : half + at + own] = value[:, share // 2 :]
        query = lax.broadcasted_iota(jnp.int32, (GROUP, GROUP), 0) // R
        block = lax.broadcasted_iota(jnp.int32, (GROUP, GROUP), 1) // R
        count = GROUP // share
        shape = (count, share // 2, GROUP)
        first = lax.broadcasted_iota(jnp.int32, shape, 0) * share // R
        ahead = lax.rem(lax.broadcasted_iota(jnp.int32, shape, 2) // R - first + GROUP // R, GROUP // R)
        for i in range(rows // GROUP):
            here = slice(i * GROUP, (i + 1) * GROUP)
            x, y = left[here], right[here]
            next_y = jnp.concatenate([y[GROUP - R :], y[: GROUP - R]], axis=0)
            gram = jnp.where(query == block, dot(x, x), dot(y, next_y))
            moved = pltpu.roll(gram, 2 * R, 1).reshape(count, share, GROUP)
            gram = gram.reshape(count, share, GROUP)
            out[i * count : (i + 1) * count, :, 2 * half :] = jnp.where(
                ahead < 2, gram[:, : share // 2], moved[:, share // 2 :]
            )

    return pl.pallas_call(
        body,
        in_specs=[VMEM] * (len(pieces) + 2),
        out_specs=VMEM,
        out_shape=jax.ShapeDtypeStruct((OWNERS, share // 2, width), jnp.float32),
        scratch_shapes=[
            pltpu.VMEM((rows, wide), mine.dtype),
            pltpu.VMEM((rows, both - wide), mine.dtype),
        ],
        compiler_params=params(),
        cost_estimate=pl.CostEstimate(
            flops=int(weight * rows * half * packed),
            bytes_accessed=int(weight * 2 * rows * packed),
            transcendentals=0,
        ),
    )(*pieces, mine, theirs)


def class_rows(place, terms):
    half = (terms.shape[2] - GROUP) // 2
    own = half // 4
    total = terms[0]
    for s in range(1, OWNERS):
        total = total + terms[s]
    products = total[:, : 2 * own] * total[:, 2 * own : half]
    products += total[:, half : half + 2 * own] * total[:, half + 2 * own : 2 * half]
    both = jnp.sum(products, axis=0, keepdims=True)
    gram = total[:, 2 * half :]
    gram = gram * pltpu.roll(gram, GROUP - R, 1)
    lanes = lax.broadcasted_iota(jnp.int32, (1, GROUP), 1)
    lefts = lax.rem(lanes // R + place[2], 2) == 0
    square = jnp.sum(jnp.where(lefts, gram, 0.0), axis=(0, 1), keepdims=True)
    square = jnp.broadcast_to(square, (1, GROUP))
    mine = jnp.concatenate([both[:, :own], square], axis=1)
    theirs = jnp.concatenate([both[:, own:], square], axis=1)
    return jnp.where(place[0] == 0, mine, theirs), jnp.where(place[0] == 0, theirs, mine)


def finish_first(place, terms):
    width = (terms.shape[2] - GROUP) // 8 + GROUP

    def body(place_ref, terms_ref, out):
        out[0:1], out[1:2] = class_rows(place_ref, terms_ref)

    return pl.pallas_call(
        body,
        in_specs=[SMEM, VMEM],
        out_specs=VMEM,
        out_shape=jax.ShapeDtypeStruct((2, width), jnp.float32),
        compiler_params=params(),
        cost_estimate=pl.CostEstimate(
            flops=10_000_000_000, bytes_accessed=4 * terms.size, transcendentals=0
        ),
    )(place, terms)


def finish(place, first_rows, terms):
    width = first_rows.shape[1]

    def body(place_ref, first_ref, terms_ref, out):
        second = class_rows(place_ref, terms_ref)
        at = lax.broadcasted_iota(jnp.int32, (CLASSES, width), 0)
        for core in range(2):
            rows = jnp.where(at == place_ref[1], first_ref[core : core + 1], second[core])
            out[core * OWNERS : (core + 1) * OWNERS] = jnp.broadcast_to(
                rows[None], (OWNERS, CLASSES, width)
            )

    return pl.pallas_call(
        body,
        in_specs=[SMEM, VMEM, VMEM],
        out_specs=VMEM,
        out_shape=jax.ShapeDtypeStruct((2 * OWNERS, CLASSES, width), jnp.float32),
        compiler_params=params(),
    )(place, first_rows, terms)


def scores_of(got, shares):
    own = got.shape[2] - GROUP
    queries = got.shape[0] // 2 // shares

    def body(got_ref, out):
        for core in range(2):
            for a in range(queries):
                first = (core * queries + a) * shares
                total = got_ref[first]
                for b in range(1, shares):
                    total = total + got_ref[first + b]
                values = total[:, :own] / jnp.sqrt(total[:, own : own + 1] + epsilon)
                for g in range(CLASSES):
                    row = 2 * (CLASSES * a + g) + core
                    out[row : row + 1, :] = values[g : g + 1]

    return pl.pallas_call(
        body,
        in_specs=[VMEM],
        out_specs=VMEM,
        out_shape=jax.ShapeDtypeStruct((2 * CLASSES * queries, own), jnp.float32),
        compiler_params=params(),
    )(got)


def on_device(hidden_acts, out_grads, query_left, query_right):
    planes = lax.axis_size(("zh", "zp"))

    def from_plane(block, ahead):
        pairs = [((z + ahead) % planes, z) for z in range(planes)]
        return lax.ppermute(block, ("zh", "zp"), pairs)

    mine = jnp.concatenate([hidden_acts, out_grads], axis=1)
    tokens = (mine, lax.ppermute(mine, "c", [(0, 1), (1, 0)]))
    wide = hidden_acts.shape[1]

    sent = pack(query_left, query_right).astype(jnp.float16)
    here = lax.all_gather(sent, "zh", axis=0, tiled=True)
    half = here.shape[0] // 2
    here = (here[:half].astype(query_left.dtype), here[half:].astype(query_left.dtype))
    there = (from_plane(here[0], 1), from_plane(here[1], -1))

    def owned(terms):
        return lax.all_to_all(terms, ("x", "y"), split_axis=0, concat_axis=0, tiled=True)

    share = 2 * half // OWNERS
    shares = R // share
    place = jnp.stack(
        [
            lax.axis_index("c"),
            lax.axis_index("zp"),
            lax.rem(lax.axis_index(("x", "y")) // shares, GROUP // R),
        ]
    ).astype(jnp.int32)

    first_terms = project(WEIGHTS[0], wide, here, *tokens)
    first = owned(first_terms)
    there, _ = lax.optimization_barrier((there, first_terms))
    second_terms, first = lax.optimization_barrier((project(WEIGHTS[1], wide, there, *tokens), first))
    second = owned(second_terms)
    sums = finish(place, finish_first(place, first), second)
    got = lax.all_to_all(sums, ("c", "x", "y"), split_axis=0, concat_axis=0, tiled=True)
    return scores_of(got, shares)


def solution(mesh):
    devices = mesh.devices
    planes = devices.shape[0] // 2
    owners = devices.shape[1]
    side = int(round(owners**0.5))
    shape = (planes // CLASSES, CLASSES, 2, side, side)
    grid = Mesh(devices.reshape(shape), ("zh", "zp", "c", "x", "y"))
    placed = P(("zh", "zp", "c"), ("x", "y"))
    return jax.shard_map(
        on_device,
        mesh=grid,
        in_specs=(placed,) * 4,
        out_specs=P(None, ("zh", "zp", "c")),
        check_vma=False,
    )
```
